1024 devices in a mesh: dp: 128 (over y, x_lo, z), mp: 8 (over x_hi, core).
Axes of the slice: x: 8 (x_hi: 4, x_lo: 2; x = x_hi * 2 + x_lo), y: 8, z: 8, core: 2. Of those that a mesh axis runs over, the one named last changes fastest.
Arguments:
- tokens: bfloat16 [256, 6144], P('dp', 'mp'), may hold values from -6 to 6
- weight_in: bfloat16 [6144, 24576], P('mp', 'dp'), may hold values from -0.078125 to 0.078125
- bias_in: float32 [24576], P('dp'), may hold values from -3 to 3
- weight_out: bfloat16 [24576, 6144], P('dp', 'mp'), may hold values from -0.0390625 to 0.0390625
- grad_out: bfloat16 [256, 6144], P('dp', 'mp'), may hold values from -6 to 6
Outputs:
- mixed: bfloat16 [256, 6144], P('dp', 'mp')
- grad_tokens: bfloat16 [256, 6144], P('dp', 'mp')
- grad_weight_in: bfloat16 [6144, 24576], P('mp', 'dp')
- grad_bias: float32 [24576], P('dp')
- grad_weight_out: bfloat16 [24576, 6144], P('dp', 'mp')
The draws below stay inside these ranges and needn't reach their ends.
All inputs are finite; a program needn't handle non-finite values.
Results may differ from the reference program's by a relative error of at most 0.0049.
Values may be sent and summed in bfloat16 or wider, within the bound.
No kernel may reach another device: no remote copies, remote signals or barrier semaphores. Data moves between devices by JAX's collectives and lax.ppermute only.
A program may use at most 32 MiB of HBM per device.

```python
import jax
import jax.numpy as jnp
from jax import lax

D = 6144
FF = 24576
TOKENS = 256


def shard_levels(rng, extent, shards, smallest, largest):
    gain = 1.0
    for axis_at, shards_of in shards:
        draws = jax.random.uniform(jax.random.fold_in(jax.random.fold_in(rng, 6), axis_at), (shards_of,), jnp.float32, smallest / len(shards), largest / len(shards))
        gain = gain * jnp.repeat(jnp.exp(draws), extent[axis_at] // shards_of).reshape((-1,) + (1,) * (len(extent) - 1 - axis_at))
    return gain


def bell_draw(rng, dims, width, limit, pieces=(), dtype=jnp.bfloat16):
    gain = shard_levels(rng, dims, pieces, -0.22, 0.18) if pieces else 1.0
    result = jax.random.normal(rng, dims, jnp.float32) * width * gain
    return jnp.minimum(jnp.maximum(result, -limit), limit).astype(dtype)


def setup_inputs(seed: int = 0) -> dict:
    arg_keys = jax.random.split(jax.random.key(seed), 6)
    return {
        "tokens": bell_draw(arg_keys[0], (TOKENS, D), 1.0, 6.0, ((0, 128), (1, 8))),
        "weight_in": bell_draw(arg_keys[1], (D, FF), D ** -0.5, 0.078125, ((0, 8), (1, 128))),
        "bias_in": bell_draw(arg_keys[2], (FF,), 0.5, 3.0, ((0, 128),), jnp.float32),
        "weight_out": bell_draw(arg_keys[3], (FF, D), FF ** -0.5, 0.0390625, ((0, 128), (1, 8))),
        "grad_out": bell_draw(arg_keys[4], (TOKENS, D), 1.0, 6.0, ((0, 128), (1, 8))),
    }


def activation(values):
    return jax.nn.gelu(values, approximate=True)

def reference(tokens, weight_in, bias_in, weight_out, grad_out):
    pre = jnp.dot(tokens, weight_in, preferred_element_type=jnp.float32) + bias_in
    acts_full, backward = jax.vjp(activation, pre)
    acts = acts_full.astype(jnp.bfloat16)
    mixed = jnp.dot(acts, weight_out, preferred_element_type=jnp.float32).astype(jnp.bfloat16)
    grad_acts = lax.dot_general(grad_out, weight_out, (((1,), (1,)), ((), ())), preferred_element_type=jnp.float32)
    grad_pre = backward(grad_acts)[0].astype(jnp.bfloat16)
    grad_weight_out = lax.dot_general(acts, grad_out, (((0,), (0,)), ((), ())), preferred_element_type=jnp.float32).astype(jnp.bfloat16)
    grad_weight_in = lax.dot_general(tokens, grad_pre, (((0,), (0,)), ((), ())), preferred_element_type=jnp.float32).astype(jnp.bfloat16)
    grad_bias = lax.optimization_barrier(jnp.sum(grad_pre.astype(jnp.float32), axis=0))
    grad_tokens = lax.dot_general(grad_pre, weight_in, (((1,), (1,)), ((), ())), preferred_element_type=jnp.float32).astype(jnp.bfloat16)
    return (mixed, grad_tokens, grad_weight_in, grad_bias, grad_weight_out)
```

```python
import jax
import jax.numpy as jnp
from jax import lax
from jax.sharding import PartitionSpec as P

BF = jnp.bfloat16
F32 = jnp.float32


def activation(values):
    return jax.nn.gelu(values, approximate=True)


def finish(pre_part, grad_part, bias_in):
    pre = pre_part + bias_in
    acts_full, backward = jax.vjp(activation, pre)
    grad_pre = backward(grad_part)[0]
    return (acts_full.astype(BF), grad_pre.astype(BF))


def exchange(blocks, axis):
    return lax.all_to_all(blocks, axis, split_axis=0, concat_axis=0, tiled=True)


def spread(block, axis):
    n = lax.axis_size(axis)
    return exchange(jnp.broadcast_to(block[None], (n, *block.shape)), axis)


def body(tokens, weight_in, bias_in, weight_out, grad_out):
    rows, width = tokens.shape
    hidden = weight_in.shape[1]
    dp, mp = lax.axis_size("dp"), lax.axis_size("mp")
    total = rows * dp
    both = spread(jnp.concatenate([tokens, grad_out], axis=1), "dp").reshape(total, 2 * width)
    all_tokens, all_grads = both[:, :width], both[:, width:]
    pre_part = jnp.dot(all_tokens, weight_in, preferred_element_type=F32)
    grad_part = lax.dot_general(
        all_grads, weight_out, (((1,), (1,)), ((), ())), preferred_element_type=F32
    )
    parts = jnp.concatenate([pre_part, grad_part], axis=1).reshape(mp, total // mp, 2 * hidden)
    share = jnp.sum(exchange(parts, "mp"), axis=0)
    acts_share, grad_pre_share = finish(share[:, :hidden], share[:, hidden:], bias_in)
    halves = spread(jnp.concatenate([acts_share, grad_pre_share], axis=1), "mp")
    halves = halves.reshape(total, 2 * hidden)
    acts, grad_pre = halves[:, :hidden], halves[:, hidden:]
    mixed_part = jnp.dot(acts, weight_out, preferred_element_type=F32)
    back_part = lax.dot_general(
        grad_pre, weight_in, (((1,), (1,)), ((), ())), preferred_element_type=F32
    )
    sums = jnp.concatenate([mixed_part, back_part], axis=1).astype(BF).reshape(dp, rows, 2 * width)
    summed = jnp.sum(exchange(sums, "dp").astype(F32), axis=0)
    mixed = summed[:, :width].astype(BF)
    grad_tokens = summed[:, width:].astype(BF)
    grad_weight_in = lax.dot_general(
        all_tokens, grad_pre, (((0,), (0,)), ((), ())), preferred_element_type=F32
    ).astype(BF)
    grad_bias = jnp.sum(grad_pre.astype(F32), axis=0)
    grad_weight_out = lax.dot_general(
        acts, all_grads, (((0,), (0,)), ((), ())), preferred_element_type=F32
    ).astype(BF)
    return (mixed, grad_tokens, grad_weight_in, grad_bias, grad_weight_out)


def solution(mesh):
    return jax.shard_map(
        body,
        mesh=mesh,
        in_specs=(P("dp", "mp"), P("mp", "dp"), P("dp"), P("dp", "mp"), P("dp", "mp")),
        out_specs=(P("dp", "mp"), P("dp", "mp"), P("mp", "dp"), P("dp"), P("dp", "mp")),
        check_vma=False,
    )
```

```python
import jax
import jax.numpy as jnp
from jax import lax
from jax.sharding import Mesh, PartitionSpec as P

BF = jnp.bfloat16
F32 = jnp.float32

AXES = {"y": 8, "xl": 2, "z": 8, "xh": 4, "core": 2}
DP, MP = ("y", "xl", "z"), ("xh", "core")


def activation(values):
    return jax.nn.gelu(values, approximate=True)


def finish(pre_part, grad_part, bias_in):
    pre = pre_part + bias_in
    acts_full, backward = jax.vjp(activation, pre)
    grad_pre = backward(grad_part)[0]
    return (acts_full.astype(BF), grad_pre.astype(BF))


def exchange(blocks, axis):
    return lax.all_to_all(blocks, axis, split_axis=0, concat_axis=0, tiled=True)


def spread(block, axis):
    n = lax.axis_size(axis)
    return exchange(jnp.broadcast_to(block[None], (n, *block.shape)), axis)


def body(tokens, weight_in, bias_in, weight_out, grad_out):
    rows, width = tokens.shape
    hidden = weight_in.shape[1]
    dp, cores = lax.axis_size(DP), lax.axis_size("core")
    total = rows * dp
    both = spread(jnp.concatenate([tokens, grad_out], axis=1), DP).reshape(total, 2 * width)
    all_tokens, all_grads = both[:, :width], both[:, width:]
    pre_part = jnp.dot(all_tokens, weight_in, preferred_element_type=F32)
    grad_part = lax.dot_general(
        all_grads, weight_out, (((1,), (1,)), ((), ())), preferred_element_type=F32
    )
    parts = jnp.concatenate([pre_part, grad_part], axis=1)
    pair = lax.all_gather(parts, "core", axis=0, tiled=False)
    half = total // cores
    mine = lax.dynamic_slice_in_dim(pair, lax.axis_index("core") * half, half, axis=1)
    chip = jnp.sum(mine, axis=0).astype(BF)
    share = jnp.sum(spread(chip, "xh").astype(F32), axis=0)
    acts_share, grad_pre_share = finish(share[:, :hidden], share[:, hidden:], bias_in)
    done = lax.all_gather(
        jnp.concatenate([acts_share, grad_pre_share], axis=1), "core", axis=0, tiled=True
    )
    acts, grad_pre = done[:, :hidden], done[:, hidden:]
    mixed_part = jnp.dot(acts, weight_out, preferred_element_type=F32)
    back_part = lax.dot_general(
        grad_pre, weight_in, (((1,), (1,)), ((), ())), preferred_element_type=F32
    )
    sums = jnp.concatenate([mixed_part, back_part], axis=1).astype(BF).reshape(dp, rows, 2 * width)
    summed = jnp.sum(exchange(sums, DP).astype(F32), axis=0)
    mixed = summed[:, :width].astype(BF)
    grad_tokens = summed[:, width:].astype(BF)
    grad_weight_in = lax.dot_general(
        all_tokens, grad_pre, (((0,), (0,)), ((), ())), preferred_element_type=F32
    ).astype(BF)
    grad_bias = jnp.sum(grad_pre.astype(F32), axis=0)
    grad_weight_out = lax.dot_general(
        acts, all_grads, (((0,), (0,)), ((), ())), preferred_element_type=F32
    ).astype(BF)
    return (mixed, grad_tokens, grad_weight_in, grad_bias, grad_weight_out)


def solution(mesh):
    fine = Mesh(mesh.devices.reshape(tuple(AXES.values())), tuple(AXES))
    return jax.shard_map(
        body,
        mesh=fine,
        in_specs=(P(DP, MP), P(MP, DP), P(DP), P(DP, MP), P(DP, MP)),
        out_specs=(P(DP, MP), P(DP, MP), P(MP, DP), P(DP), P(DP, MP)),
        check_vma=False,
    )
```

```python
import jax
import jax.numpy as jnp
from jax import lax
from jax.sharding import Mesh, PartitionSpec as P

BF = jnp.bfloat16
F32 = jnp.float32

AXES = {"yh": 4, "yl": 2, "xl": 2, "zh": 4, "zl": 2, "xh": 4, "core": 2}
DP, MP = ("yh", "yl", "xl", "zh", "zl"), ("xh", "core")
FAR, NEAR = ("yh", "zh"), ("yl", "xl", "zl")


def activation(values):
    return jax.nn.gelu(values, approximate=True)


def finish(pre_part, grad_part, bias_in):
    pre = pre_part + bias_in
    acts_full, backward = jax.vjp(activation, pre)
    grad_pre = backward(grad_part)[0]
    return (acts_full.astype(BF), grad_pre.astype(BF))


def exchange(blocks, axis):
    return lax.all_to_all(blocks, axis, split_axis=0, concat_axis=0, tiled=True)


def spread(block, axis):
    n = lax.axis_size(axis)
    return exchange(jnp.broadcast_to(block[None], (n, *block.shape)), axis)


def body(tokens, weight_in, bias_in, weight_out, grad_out):
    rows, width = tokens.shape
    hidden = weight_in.shape[1]
    dp, cores = lax.axis_size(DP), lax.axis_size("core")
    total = rows * dp
    far = lax.axis_size(FAR)
    few = spread(jnp.concatenate([tokens, grad_out], axis=1), FAR).reshape(far * rows, 2 * width)
    both = spread(few, NEAR).reshape(total, 2 * width)
    all_tokens, all_grads = both[:, :width], both[:, width:]
    pre_part = jnp.dot(all_tokens, weight_in, preferred_element_type=F32)
    grad_part = lax.dot_general(
        all_grads, weight_out, (((1,), (1,)), ((), ())), preferred_element_type=F32
    )
    parts = jnp.concatenate([pre_part, grad_part], axis=1)
    pair = lax.all_gather(parts, "core", axis=0, tiled=False)
    half = total // cores
    mine = lax.dynamic_slice_in_dim(pair, lax.axis_index("core") * half, half, axis=1)
    chip = jnp.sum(mine, axis=0).astype(BF)
    share = jnp.sum(spread(chip, "xh").astype(F32), axis=0)
    acts_share, grad_pre_share = finish(share[:, :hidden], share[:, hidden:], bias_in)
    done = lax.all_gather(
        jnp.concatenate([acts_share, grad_pre_share], axis=1), "core", axis=0, tiled=True
    )
    acts, grad_pre = done[:, :hidden], done[:, hidden:]
    mixed_part = jnp.dot(acts, weight_out, preferred_element_type=F32)
    back_part = lax.dot_general(
        grad_pre, weight_in, (((1,), (1,)), ((), ())), preferred_element_type=F32
    )
    sums = jnp.concatenate([mixed_part, back_part], axis=1).astype(BF)
    near_sums = exchange(sums.reshape(dp // far, far * rows, 2 * width), NEAR).astype(F32)
    far_sums = jnp.sum(near_sums, axis=0).reshape(far, rows, 2 * width)
    summed = jnp.sum(exchange(far_sums, FAR), axis=0)
    mixed = summed[:, :width].astype(BF)
    grad_tokens = summed[:, width:].astype(BF)
    grad_weight_in = lax.dot_general(
        all_tokens, grad_pre, (((0,), (0,)), ((), ())), preferred_element_type=F32
    ).astype(BF)
    grad_bias = jnp.sum(grad_pre.astype(F32), axis=0)
    grad_weight_out = lax.dot_general(
        acts, all_grads, (((0,), (0,)), ((), ())), preferred_element_type=F32
    ).astype(BF)
    return (mixed, grad_tokens, grad_weight_in, grad_bias, grad_weight_out)


def solution(mesh):
    fine = Mesh(mesh.devices.reshape(tuple(AXES.values())), tuple(AXES))
    return jax.shard_map(
        body,
        mesh=fine,
        in_specs=(P(DP, MP), P(MP, DP), P(DP), P(DP, MP), P(DP, MP)),
        out_specs=(P(DP, MP), P(DP, MP), P(MP, DP), P(DP), P(DP, MP)),
        check_vma=False,
    )
```

```python
import jax
import jax.numpy as jnp
from jax import lax
from jax.sharding import Mesh, PartitionSpec as P

BF = jnp.bfloat16
F32 = jnp.float32

AXES = {"yh": 4, "yl": 2, "xl": 2, "zh": 4, "zl": 2, "xh": 4, "core": 2}
DP, MP = ("yh", "yl", "xl", "zh", "zl"), ("xh", "core")
FAR, NEAR = ("yh", "zh"), ("yl", "zl")
SWAP = [(0, 1), (1, 0)]


def activation(values):
    return jax.nn.gelu(values, approximate=True)


def finish(pre_part, grad_part, bias_in):
    pre = pre_part + bias_in
    acts_full, backward = jax.vjp(activation, pre)
    grad_pre = backward(grad_part)[0]
    return (acts_full.astype(BF), grad_pre.astype(BF))


def exchange(blocks, axis):
    return lax.all_to_all(blocks, axis, split_axis=0, concat_axis=0, tiled=True)


def spread(block, axis):
    n = lax.axis_size(axis)
    return exchange(jnp.broadcast_to(block[None], (n, *block.shape)), axis)


def swap(block):
    return lax.ppermute(block, "xl", SWAP)


def dot(a, b, over):
    return lax.dot_general(a, b, ((over[:1], over[1:]), ((), ())), preferred_element_type=F32)


def body(tokens, weight_in, bias_in, weight_out, grad_out):
    rows, width = tokens.shape
    hidden = weight_in.shape[1]
    far, near, cores = lax.axis_size(FAR), lax.axis_size(NEAR), lax.axis_size("core")
    total = near * far * rows

    next_in, next_out = swap(weight_in.T), swap(weight_out)
    w_out = jnp.concatenate([weight_out, next_out], axis=0)
    bias = jnp.concatenate([bias_in, swap(bias_in)])

    few = spread(jnp.concatenate([tokens, grad_out], axis=1), FAR).reshape(far * rows, 2 * width)
    few, next_in = lax.optimization_barrier((few, next_in))
    w_in = jnp.concatenate([weight_in.T, next_in], axis=0)
    both = spread(few, NEAR).reshape(total, 2 * width)
    parts = jnp.concatenate(
        [dot(both[:, :width], w_in, (1, 1)), dot(both[:, width:], w_out, (1, 1))], axis=1
    )
    pair = lax.all_gather(parts, "core", axis=0, tiled=False)
    half = total // cores
    mine = lax.dynamic_slice_in_dim(pair, lax.axis_index("core") * half, half, axis=1)
    chip = jnp.sum(mine, axis=0).astype(BF)
    share = jnp.sum(spread(chip, "xh").astype(F32), axis=0)
    acts_share, grad_pre_share = finish(share[:, : 2 * hidden], share[:, 2 * hidden :], bias)
    done = lax.all_gather(
        jnp.concatenate([acts_share, grad_pre_share], axis=1), "core", axis=0, tiled=True
    )
    acts, grad_pre = done[:, : 2 * hidden], done[:, 2 * hidden :]

    sums = jnp.concatenate([dot(acts, w_out, (1, 0)), dot(grad_pre, w_in, (1, 0))], axis=1)
    near_sums = exchange(sums.astype(BF).reshape(near, far * rows, 2 * width), NEAR)
    far_sums = jnp.sum(near_sums.astype(F32), axis=0).reshape(far, rows, 2 * width)
    summed = jnp.sum(exchange(far_sums, FAR), axis=0)
    mixed = summed[:, :width].astype(BF)
    grad_tokens = summed[:, width:].astype(BF)

    theirs = swap(jnp.concatenate([both, acts[:, hidden:], grad_pre[:, hidden:]], axis=1))
    theirs, _ = lax.optimization_barrier((theirs, near_sums))
    all_both = jnp.concatenate([both, theirs[:, : 2 * width]], axis=0)
    all_acts = jnp.concatenate([acts[:, :hidden], theirs[:, 2 * width : 2 * width + hidden]], axis=0)
    all_pre = jnp.concatenate([grad_pre[:, :hidden], theirs[:, 2 * width + hidden :]], axis=0)
    grad_weight_in = dot(all_both[:, :width], all_pre, (0, 0)).astype(BF)
    grad_bias = jnp.sum(all_pre.astype(F32), axis=0)
    grad_weight_out = dot(all_acts, all_both[:, width:], (0, 0)).astype(BF)
    return (mixed, grad_tokens, grad_weight_in, grad_bias, grad_weight_out)


def solution(mesh):
    fine = Mesh(mesh.devices.reshape(tuple(AXES.values())), tuple(AXES))
    return jax.shard_map(
        body,
        mesh=fine,
        in_specs=(P(DP, MP), P(MP, DP), P(DP), P(DP, MP), P(DP, MP)),
        out_specs=(P(DP, MP), P(DP, MP), P(MP, DP), P(DP), P(DP, MP)),
        check_vma=False,
    )
```

```python
import jax
import jax.numpy as jnp
from jax import lax
from jax.sharding import Mesh, PartitionSpec as P

BF = jnp.bfloat16
F32 = jnp.float32

AXES = {"yh": 4, "yl": 2, "xl": 2, "zh": 4, "zl": 2, "xh": 4, "core": 2}
DP, MP = ("yh", "yl", "xl", "zh", "zl"), ("xh", "core")
FAR, NEAR = ("yh", "zh"), ("yl", "zl")
SWAP = [(0, 1), (1, 0)]


def activation(values):
    return jax.nn.gelu(values, approximate=True)


def finish(pre_part, grad_part, bias_in):
    pre = pre_part + bias_in
    acts_full, backward = jax.vjp(activation, pre)
    grad_pre = backward(grad_part)[0]
    return (acts_full.astype(BF), grad_pre.astype(BF))


def exchange(blocks, axis):
    return lax.all_to_all(blocks, axis, split_axis=0, concat_axis=0, tiled=True)


def spread(block, axis):
    n = lax.axis_size(axis)
    return exchange(jnp.broadcast_to(block[None], (n, *block.shape)), axis)


def swap(block):
    return lax.ppermute(block, "xl", SWAP)


def dot(a, b, over):
    return lax.dot_general(a, b, ((over[:1], over[1:]), ((), ())), preferred_element_type=F32)


def body(tokens, weight_in, bias_in, weight_out, grad_out):
    rows, width = tokens.shape
    hidden = weight_in.shape[1]
    far, near, cores = lax.axis_size(FAR), lax.axis_size(NEAR), lax.axis_size("core")
    total = near * far * rows

    w_in = jnp.concatenate([weight_in.T, swap(weight_in.T)], axis=0)
    w_out = jnp.concatenate([weight_out, swap(weight_out)], axis=0)
    bias = jnp.concatenate([bias_in, swap(bias_in)])

    both = spread(jnp.concatenate([tokens, grad_out], axis=1), NEAR + FAR).reshape(total, 2 * width)
    parts = jnp.concatenate(
        [dot(both[:, :width], w_in, (1, 1)), dot(both[:, width:], w_out, (1, 1))], axis=1
    )
    pair = lax.all_gather(parts, "core", axis=0, tiled=False)
    half = total // cores
    mine = lax.dynamic_slice_in_dim(pair, lax.axis_index("core") * half, half, axis=1)
    chip = jnp.sum(mine, axis=0).astype(BF)
    share = jnp.sum(spread(chip, "xh").astype(F32), axis=0)
    acts_share, grad_pre_share = finish(share[:, : 2 * hidden], share[:, 2 * hidden :], bias)
    done = lax.all_gather(
        jnp.concatenate([acts_share, grad_pre_share], axis=1), "core", axis=0, tiled=True
    )
    acts, grad_pre = done[:, : 2 * hidden], done[:, 2 * hidden :]

    sums = jnp.concatenate([dot(acts, w_out, (1, 0)), dot(grad_pre, w_in, (1, 0))], axis=1)
    near_sums = exchange(sums.astype(BF).reshape(near, far * rows, 2 * width), NEAR)
    far_sums = jnp.sum(near_sums.astype(F32), axis=0).reshape(far, rows, 2 * width)
    summed = jnp.sum(exchange(far_sums, FAR), axis=0)
    mixed = summed[:, :width].astype(BF)
    grad_tokens = summed[:, width:].astype(BF)

    theirs = swap(jnp.concatenate([both, acts[:, hidden:], grad_pre[:, hidden:]], axis=1))
    theirs, _ = lax.optimization_barrier((theirs, near_sums))
    all_both = jnp.concatenate([both, theirs[:, : 2 * width]], axis=0)
    all_acts = jnp.concatenate([acts[:, :hidden], theirs[:, 2 * width : 2 * width + hidden]], axis=0)
    all_pre = jnp.concatenate([grad_pre[:, :hidden], theirs[:, 2 * width + hidden :]], axis=0)
    grad_weight_in = dot(all_both[:, :width], all_pre, (0, 0)).astype(BF)
    grad_bias = jnp.sum(all_pre.astype(F32), axis=0)
    grad_weight_out = dot(all_acts, all_both[:, width:], (0, 0)).astype(BF)
    return (mixed, grad_tokens, grad_weight_in, grad_bias, grad_weight_out)


def solution(mesh):
    fine = Mesh(mesh.devices.reshape(tuple(AXES.values())), tuple(AXES))
    return jax.shard_map(
        body,
        mesh=fine,
        in_specs=(P(DP, MP), P(MP, DP), P(DP), P(DP, MP), P(DP, MP)),
        out_specs=(P(DP, MP), P(DP, MP), P(MP, DP), P(DP), P(DP, MP)),
        check_vma=False,
    )
```

```python
import jax
import jax.numpy as jnp
from jax import lax
from jax.sharding import Mesh, PartitionSpec as P

BF = jnp.bfloat16
F32 = jnp.float32

AXES = {"y": 8, "xl": 2, "z": 8, "xh": 4, "core": 2}
DP, MP = ("y", "xl", "z"), ("xh", "core")
YZ = ("y", "z")
SWAP = [(0, 1), (1, 0)]


def activation(values):
    return jax.nn.gelu(values, approximate=True)


def finish(pre_part, grad_part, bias_in):
    pre = pre_part + bias_in
    acts_full, backward = jax.vjp(activation, pre)
    grad_pre = backward(grad_part)[0]
    return (acts_full.astype(BF), grad_pre.astype(BF))


def exchange(blocks, axis):
    return lax.all_to_all(blocks, axis, split_axis=0, concat_axis=0, tiled=True)


def spread(block, axis):
    n = lax.axis_size(axis)
    return exchange(jnp.broadcast_to(block[None], (n, *block.shape)), axis)


def swap(block):
    return lax.ppermute(block, "xl", SWAP)


def dot(a, b, over):
    return lax.dot_general(a, b, ((over[:1], over[1:]), ((), ())), preferred_element_type=F32)


def body(tokens, weight_in, bias_in, weight_out, grad_out):
    rows, width = tokens.shape
    hidden = weight_in.shape[1]
    owners, cores = lax.axis_size(YZ), lax.axis_size("core")
    total = owners * rows

    w_in = jnp.concatenate([weight_in.T, swap(weight_in.T)], axis=0)
    w_out = jnp.concatenate([weight_out, swap(weight_out)], axis=0)
    bias = jnp.concatenate([bias_in, swap(bias_in)])

    both = spread(jnp.concatenate([tokens, grad_out], axis=1), YZ).reshape(total, 2 * width)
    parts = jnp.concatenate(
        [dot(both[:, :width], w_in, (1, 1)), dot(both[:, width:], w_out, (1, 1))], axis=1
    )
    pair = lax.all_gather(parts, "core", axis=0, tiled=False)
    half = total // cores
    mine = lax.dynamic_slice_in_dim(pair, lax.axis_index("core") * half, half, axis=1)
    chip = jnp.sum(mine, axis=0).astype(BF)
    share = jnp.sum(spread(chip, "xh").astype(F32), axis=0)
    acts_share, grad_pre_share = finish(share[:, : 2 * hidden], share[:, 2 * hidden :], bias)
    done = lax.all_gather(
        jnp.concatenate([acts_share, grad_pre_share], axis=1), "core", axis=0, tiled=True
    )
    acts, grad_pre = done[:, : 2 * hidden], done[:, 2 * hidden :]

    sums = jnp.concatenate([dot(acts, w_out, (1, 0)), dot(grad_pre, w_in, (1, 0))], axis=1)
    summed = jnp.sum(exchange(sums.astype(BF).reshape(owners, rows, 2 * width), YZ).astype(F32), axis=0)
    mixed = summed[:, :width].astype(BF)
    grad_tokens = summed[:, width:].astype(BF)

    theirs = swap(jnp.concatenate([both, acts[:, hidden:], grad_pre[:, hidden:]], axis=1))
    all_both = jnp.concatenate([both, theirs[:, : 2 * width]], axis=0)
    all_acts = jnp.concatenate([acts[:, :hidden], theirs[:, 2 * width : 2 * width + hidden]], axis=0)
    all_pre = jnp.concatenate([grad_pre[:, :hidden], theirs[:, 2 * width + hidden :]], axis=0)
    grad_weight_in = dot(all_both[:, :width], all_pre, (0, 0)).astype(BF)
    grad_bias = jnp.sum(all_pre.astype(F32), axis=0)
    grad_weight_out = dot(all_acts, all_both[:, width:], (0, 0)).astype(BF)
    return (mixed, grad_tokens, grad_weight_in, grad_bias, grad_weight_out)


def solution(mesh):
    fine = Mesh(mesh.devices.reshape(tuple(AXES.values())), tuple(AXES))
    return jax.shard_map(
        body,
        mesh=fine,
        in_specs=(P(DP, MP), P(MP, DP), P(DP), P(DP, MP), P(DP, MP)),
        out_specs=(P(DP, MP), P(DP, MP), P(MP, DP), P(DP), P(DP, MP)),
        check_vma=False,
    )
```

```python
import jax
import jax.numpy as jnp
from jax import lax
from jax.sharding import Mesh, PartitionSpec as P

BF = jnp.bfloat16
F32 = jnp.float32

AXES = {"y": 8, "xl": 2, "z": 8, "xh": 4, "core": 2}
DP, MP = ("y", "xl", "z"), ("xh", "core")
YZ = ("y", "z")
SWAP = [(0, 1), (1, 0)]


def activation(values):
    return jax.nn.gelu(values, approximate=True)


def finish(pre_part, grad_part, bias_in):
    pre = pre_part + bias_in
    acts_full, backward = jax.vjp(activation, pre)
    grad_pre = backward(grad_part)[0]
    return (acts_full.astype(BF), grad_pre.astype(BF))


def exchange(blocks, axis):
    return lax.all_to_all(blocks, axis, split_axis=0, concat_axis=0, tiled=True)


def spread(block, axis):
    n = lax.axis_size(axis)
    return exchange(jnp.broadcast_to(block[None], (n, *block.shape)), axis)


def swap(block):
    return lax.ppermute(block, "xl", SWAP)


def dot(a, b, over):
    return lax.dot_general(a, b, ((over[:1], over[1:]), ((), ())), preferred_element_type=F32)


def body(tokens, weight_in, bias_in, weight_out, grad_out):
    rows, width = tokens.shape
    hidden = weight_in.shape[1]
    owners, cores = lax.axis_size(YZ), lax.axis_size("core")
    total = owners * rows

    w_in = jnp.concatenate([weight_in.T, swap(weight_in.T)], axis=0)
    w_out = jnp.concatenate([weight_out, swap(weight_out)], axis=0)
    bias = jnp.concatenate([bias_in, swap(bias_in)])

    every = spread(jnp.concatenate([tokens, grad_out], axis=1), ("xl", *YZ)).reshape(2, total, 2 * width)
    here = lax.axis_index("xl")
    both = lax.dynamic_index_in_dim(every, here, 0, keepdims=False)
    other = lax.dynamic_index_in_dim(every, 1 - here, 0, keepdims=False)
    parts = jnp.concatenate(
        [dot(both[:, :width], w_in, (1, 1)), dot(both[:, width:], w_out, (1, 1))], axis=1
    )
    pair = lax.all_gather(parts, "core", axis=0, tiled=False)
    half = total // cores
    mine = lax.dynamic_slice_in_dim(pair, lax.axis_index("core") * half, half, axis=1)
    chip = jnp.sum(mine, axis=0).astype(BF)
    share = jnp.sum(spread(chip, "xh").astype(F32), axis=0)
    acts_share, grad_pre_share = finish(share[:, : 2 * hidden], share[:, 2 * hidden :], bias)
    done = lax.all_gather(
        jnp.concatenate([acts_share, grad_pre_share], axis=1), "core", axis=0, tiled=True
    )
    acts, grad_pre = done[:, : 2 * hidden], done[:, 2 * hidden :]

    sums = jnp.concatenate([dot(acts, w_out, (1, 0)), dot(grad_pre, w_in, (1, 0))], axis=1)
    summed = jnp.sum(exchange(sums.astype(BF).reshape(owners, rows, 2 * width), YZ).astype(F32), axis=0)
    mixed = summed[:, :width].astype(BF)
    grad_tokens = summed[:, width:].astype(BF)

    theirs = swap(jnp.concatenate([acts[:, hidden:], grad_pre[:, hidden:]], axis=1))
    all_both = jnp.concatenate([both, other], axis=0)
    all_acts = jnp.concatenate([acts[:, :hidden], theirs[:, :hidden]], axis=0)
    all_pre = jnp.concatenate([grad_pre[:, :hidden], theirs[:, hidden:]], axis=0)
    grad_weight_in = dot(all_both[:, :width], all_pre, (0, 0)).astype(BF)
    grad_bias = jnp.sum(all_pre.astype(F32), axis=0)
    grad_weight_out = dot(all_acts, all_both[:, width:], (0, 0)).astype(BF)
    return (mixed, grad_tokens, grad_weight_in, grad_bias, grad_weight_out)


def solution(mesh):
    fine = Mesh(mesh.devices.reshape(tuple(AXES.values())), tuple(AXES))
    return jax.shard_map(
        body,
        mesh=fine,
        in_specs=(P(DP, MP), P(MP, DP), P(DP), P(DP, MP), P(DP, MP)),
        out_specs=(P(DP, MP), P(DP, MP), P(MP, DP), P(DP), P(DP, MP)),
        check_vma=False,
    )
```

```python
import jax
import jax.numpy as jnp
from jax import lax
from jax.sharding import Mesh, PartitionSpec as P

BF = jnp.bfloat16
F32 = jnp.float32

AXES = {"y": 8, "xl": 2, "z": 8, "xh": 4, "core": 2}
DP, MP = ("y", "xl", "z"), ("xh", "core")
YZ = ("y", "z")
SWAP = [(0, 1), (1, 0)]


def activation(values):
    return jax.nn.gelu(values, approximate=True)


def finish(pre_part, grad_part, bias_in):
    pre = pre_part + bias_in
    acts_full, backward = jax.vjp(activation, pre)
    grad_pre = backward(grad_part)[0]
    return (acts_full.astype(BF), grad_pre.astype(BF))


def exchange(blocks, axis):
    return lax.all_to_all(blocks, axis, split_axis=0, concat_axis=0, tiled=True)


def spread(block, axis):
    n = lax.axis_size(axis)
    return exchange(jnp.broadcast_to(block[None], (n, *block.shape)), axis)


def swap(block):
    return lax.ppermute(block, "xl", SWAP)


def dot(a, b, over):
    return lax.dot_general(a, b, ((over[:1], over[1:]), ((), ())), preferred_element_type=F32)


def body(tokens, weight_in, bias_in, weight_out, grad_out):
    rows, width = tokens.shape
    hidden = weight_in.shape[1]
    owners, cores = lax.axis_size(YZ), lax.axis_size("core")
    total = owners * rows

    w_in = jnp.concatenate([weight_in.T, swap(weight_in.T)], axis=0)
    w_out = jnp.concatenate([weight_out, swap(weight_out)], axis=0)
    bias = jnp.concatenate([bias_in, swap(bias_in)])

    both = spread(jnp.concatenate([tokens, grad_out], axis=1), YZ).reshape(total, 2 * width)
    parts = jnp.concatenate(
        [dot(both[:, :width], w_in, (1, 1)), dot(both[:, width:], w_out, (1, 1))], axis=1
    )
    pair = lax.all_gather(parts, "core", axis=0, tiled=False)
    half = total // cores
    mine = lax.dynamic_slice_in_dim(pair, lax.axis_index("core") * half, half, axis=1)
    chip = jnp.sum(mine, axis=0).astype(BF)
    share = jnp.sum(spread(chip, "xh").astype(F32), axis=0)
    acts_share, grad_pre_share = finish(share[:, : 2 * hidden], share[:, 2 * hidden :], bias)
    done = lax.all_gather(
        jnp.concatenate([acts_share, grad_pre_share], axis=1), "core", axis=0, tiled=True
    )
    acts, grad_pre = done[:, : 2 * hidden], done[:, 2 * hidden :]

    sums = jnp.concatenate([dot(acts, w_out, (1, 0)), dot(grad_pre, w_in, (1, 0))], axis=1)
    summed = jnp.sum(exchange(sums.astype(BF).reshape(owners, rows, 2 * width), YZ).astype(F32), axis=0)
    mixed = summed[:, :width].astype(BF)
    grad_tokens = summed[:, width:].astype(BF)

    their_tokens = swap(jnp.concatenate([both[:, :width], grad_pre[:, hidden:]], axis=1))
    their_grads = swap(jnp.concatenate([both[:, width:], acts[:, hidden:]], axis=1))
    all_pre = jnp.concatenate([grad_pre[:, :hidden], their_tokens[:, width:]], axis=0)
    all_acts = jnp.concatenate([acts[:, :hidden], their_grads[:, width:]], axis=0)
    all_tokens = jnp.concatenate([both[:, :width], their_tokens[:, :width]], axis=0)
    all_grads = jnp.concatenate([both[:, width:], their_grads[:, :width]], axis=0)
    grad_weight_in = dot(all_tokens, all_pre, (0, 0)).astype(BF)
    grad_bias = jnp.sum(all_pre.astype(F32), axis=0)
    grad_weight_out = dot(all_acts, all_grads, (0, 0)).astype(BF)
    return (mixed, grad_tokens, grad_weight_in, grad_bias, grad_weight_out)


def solution(mesh):
    fine = Mesh(mesh.devices.reshape(tuple(AXES.values())), tuple(AXES))
    return jax.shard_map(
        body,
        mesh=fine,
        in_specs=(P(DP, MP), P(MP, DP), P(DP), P(DP, MP), P(DP, MP)),
        out_specs=(P(DP, MP), P(DP, MP), P(MP, DP), P(DP), P(DP, MP)),
        check_vma=False,
    )
```

```python
import jax
import jax.numpy as jnp
from jax import lax
from jax.sharding import Mesh, PartitionSpec as P

BF = jnp.bfloat16
F32 = jnp.float32

AXES = {"y": 8, "xl": 2, "z": 8, "xh": 4, "core": 2}
DP, MP = ("y", "xl", "z"), ("xh", "core")
YZ = ("y", "z")
SWAP = [(0, 1), (1, 0)]


def activation(values):
    return jax.nn.gelu(values, approximate=True)


def finish(pre_part, grad_part, bias_in):
    pre = pre_part + bias_in
    acts_full, backward = jax.vjp(activation, pre)
    grad_pre = backward(grad_part)[0]
    return (acts_full.astype(BF), grad_pre.astype(BF))


def exchange(blocks, axis):
    return lax.all_to_all(blocks, axis, split_axis=0, concat_axis=0, tiled=True)


def spread(block, axis):
    n = lax.axis_size(axis)
    return exchange(jnp.broadcast_to(block[None], (n, *block.shape)), axis)


def swap(block):
    return lax.ppermute(block, "xl", SWAP)


def dot(a, b, over):
    return lax.dot_general(a, b, ((over[:1], over[1:]), ((), ())), preferred_element_type=F32)


def body(tokens, weight_in, bias_in, weight_out, grad_out):
    rows, width = tokens.shape
    hidden = weight_in.shape[1]
    owners, cores = lax.axis_size(YZ), lax.axis_size("core")
    total = owners * rows

    w_in = jnp.concatenate([weight_in.T, swap(weight_in.T)], axis=0)
    w_out = jnp.concatenate([weight_out, swap(weight_out)], axis=0)
    bias = jnp.concatenate([bias_in, swap(bias_in)])

    both = spread(jnp.concatenate([tokens, grad_out], axis=1), YZ).reshape(total, 2 * width)
    parts = jnp.concatenate(
        [dot(both[:, :width], w_in, (1, 1)), dot(both[:, width:], w_out, (1, 1))], axis=1
    )
    pair = lax.all_gather(parts, "core", axis=0, tiled=False)
    half = total // cores
    mine = lax.dynamic_slice_in_dim(pair, lax.axis_index("core") * half, half, axis=1)
    share = jnp.sum(mine, axis=0)
    chip, chips = share.astype(BF), lax.axis_size("xh")
    for step in (2, 1, 3):
        perm = [(i, (i + step) % chips) for i in range(chips)]
        share = share + lax.ppermute(chip, "xh", perm).astype(F32)
    acts_share, grad_pre_share = finish(share[:, : 2 * hidden], share[:, 2 * hidden :], bias)
    done = lax.all_gather(
        jnp.concatenate([acts_share, grad_pre_share], axis=1), "core", axis=0, tiled=True
    )
    acts, grad_pre = done[:, : 2 * hidden], done[:, 2 * hidden :]

    sums = jnp.concatenate([dot(acts, w_out, (1, 0)), dot(grad_pre, w_in, (1, 0))], axis=1)
    summed = jnp.sum(exchange(sums.astype(BF).reshape(owners, rows, 2 * width), YZ).astype(F32), axis=0)
    mixed = summed[:, :width].astype(BF)
    grad_tokens = summed[:, width:].astype(BF)

    their_tokens = swap(jnp.concatenate([both[:, :width], grad_pre[:, hidden:]], axis=1))
    their_grads = swap(jnp.concatenate([both[:, width:], acts[:, hidden:]], axis=1))
    all_pre = jnp.concatenate([grad_pre[:, :hidden], their_tokens[:, width:]], axis=0)
    all_acts = jnp.concatenate([acts[:, :hidden], their_grads[:, width:]], axis=0)
    all_tokens = jnp.concatenate([both[:, :width], their_tokens[:, :width]], axis=0)
    all_grads = jnp.concatenate([both[:, width:], their_grads[:, :width]], axis=0)
    grad_weight_in = dot(all_tokens, all_pre, (0, 0)).astype(BF)
    grad_bias = jnp.sum(all_pre.astype(F32), axis=0)
    grad_weight_out = dot(all_acts, all_grads, (0, 0)).astype(BF)
    return (mixed, grad_tokens, grad_weight_in, grad_bias, grad_weight_out)


def solution(mesh):
    fine = Mesh(mesh.devices.reshape(tuple(AXES.values())), tuple(AXES))
    return jax.shard_map(
        body,
        mesh=fine,
        in_specs=(P(DP, MP), P(MP, DP), P(DP), P(DP, MP), P(DP, MP)),
        out_specs=(P(DP, MP), P(DP, MP), P(MP, DP), P(DP), P(DP, MP)),
        check_vma=False,
    )
```

```python
import jax
import jax.numpy as jnp
from jax import lax
from jax.sharding import Mesh, PartitionSpec as P

BF = jnp.bfloat16
F32 = jnp.float32

AXES = {"y": 8, "xl": 2, "z": 8, "xh": 4, "core": 2}
DP, MP = ("y", "xl", "z"), ("xh", "core")
YZ = ("y", "z")
SWAP = [(0, 1), (1, 0)]


def activation(values):
    return jax.nn.gelu(values, approximate=True)


def finish(pre_part, grad_part, bias_in):
    pre = pre_part + bias_in
    acts_full, backward = jax.vjp(activation, pre)
    grad_pre = backward(grad_part)[0]
    return (acts_full.astype(BF), grad_pre.astype(BF))


def exchange(blocks, axis):
    return lax.all_to_all(blocks, axis, split_axis=0, concat_axis=0, tiled=True)


def spread(block, axis):
    n = lax.axis_size(axis)
    return exchange(jnp.broadcast_to(block[None], (n, *block.shape)), axis)


def swap(block):
    return lax.ppermute(block, "xl", SWAP)


def dot(a, b, over):
    return lax.dot_general(a, b, ((over[:1], over[1:]), ((), ())), preferred_element_type=F32)


def body(tokens, weight_in, bias_in, weight_out, grad_out):
    rows, width = tokens.shape
    hidden = weight_in.shape[1]
    owners, cores = lax.axis_size(YZ), lax.axis_size("core")
    total = owners * rows

    w_in = jnp.concatenate([weight_in.T, swap(weight_in.T)], axis=0)
    w_out = jnp.concatenate([weight_out, swap(weight_out)], axis=0)

    both = spread(jnp.concatenate([tokens, grad_out], axis=1), YZ).reshape(total, 2 * width)
    parts = jnp.concatenate(
        [dot(both[:, :width], w_in, (1, 1)), dot(both[:, width:], w_out, (1, 1))], axis=1
    )
    pair = lax.all_gather(parts, "core", axis=0, tiled=False)
    half = total // cores
    mine = lax.dynamic_slice_in_dim(pair, lax.axis_index("core") * half, half, axis=1)
    share = jnp.sum(mine, axis=0)
    chip, chips = share.astype(BF), lax.axis_size("xh")
    for step in (1, 2, 3):
        perm = [(i, (i + step) % chips) for i in range(chips)]
        share = share + lax.ppermute(chip, "xh", perm).astype(F32)
    next_bias, _ = lax.optimization_barrier((bias_in, chip))
    bias = jnp.concatenate([bias_in, swap(next_bias)])
    acts_share, grad_pre_share = finish(share[:, : 2 * hidden], share[:, 2 * hidden :], bias)
    done = lax.all_gather(
        jnp.concatenate([acts_share, grad_pre_share], axis=1), "core", axis=0, tiled=True
    )
    acts, grad_pre = done[:, : 2 * hidden], done[:, 2 * hidden :]

    sums = jnp.concatenate([dot(acts, w_out, (1, 0)), dot(grad_pre, w_in, (1, 0))], axis=1)
    summed = jnp.sum(exchange(sums.astype(BF).reshape(owners, rows, 2 * width), YZ).astype(F32), axis=0)
    mixed = summed[:, :width].astype(BF)
    grad_tokens = summed[:, width:].astype(BF)

    their_tokens = swap(jnp.concatenate([both[:, :width], grad_pre[:, hidden:]], axis=1))
    their_grads = swap(jnp.concatenate([both[:, width:], acts[:, hidden:]], axis=1))
    all_pre = jnp.concatenate([grad_pre[:, :hidden], their_tokens[:, width:]], axis=0)
    all_tokens = jnp.concatenate([both[:, :width], their_tokens[:, :width]], axis=0)
    grad_weight_in = dot(all_tokens, all_pre, (0, 0)).astype(BF)
    grad_bias = jnp.sum(all_pre.astype(F32), axis=0)
    their_grads, grad_weight_in, grad_bias = lax.optimization_barrier(
        (their_grads, grad_weight_in, grad_bias)
    )
    all_acts = jnp.concatenate([acts[:, :hidden], their_grads[:, width:]], axis=0)
    all_grads = jnp.concatenate([both[:, width:], their_grads[:, :width]], axis=0)
    grad_weight_out = dot(all_acts, all_grads, (0, 0)).astype(BF)
    return (mixed, grad_tokens, grad_weight_in, grad_bias, grad_weight_out)


def solution(mesh):
    fine = Mesh(mesh.devices.reshape(tuple(AXES.values())), tuple(AXES))
    return jax.shard_map(
        body,
        mesh=fine,
        in_specs=(P(DP, MP), P(MP, DP), P(DP), P(DP, MP), P(DP, MP)),
        out_specs=(P(DP, MP), P(DP, MP), P(MP, DP), P(DP), P(DP, MP)),
        check_vma=False,
    )
```

```python
import jax
import jax.numpy as jnp
from jax import lax
from jax.sharding import Mesh, PartitionSpec as P

BF = jnp.bfloat16
F32 = jnp.float32

AXES = {"y": 8, "xl": 2, "z": 8, "xh": 4, "core": 2}
DP, MP = ("y", "xl", "z"), ("xh", "core")
YZ = ("y", "z")
SWAP = [(0, 1), (1, 0)]


def activation(values):
    return jax.nn.gelu(values, approximate=True)


def finish(pre_part, grad_part, bias_in):
    pre = pre_part + bias_in
    acts_full, backward = jax.vjp(activation, pre)
    grad_pre = backward(grad_part)[0]
    return (acts_full.astype(BF), grad_pre.astype(BF))


def exchange(blocks, axis):
    return lax.all_to_all(blocks, axis, split_axis=0, concat_axis=0, tiled=True)


def spread(block, axis):
    n = lax.axis_size(axis)
    return exchange(jnp.broadcast_to(block[None], (n, *block.shape)), axis)


def swap(block):
    return lax.ppermute(block, "xl", SWAP)


def dot(a, b, over):
    return lax.dot_general(a, b, ((over[:1], over[1:]), ((), ())), preferred_element_type=F32)


def body(tokens, weight_in, bias_in, weight_out, grad_out):
    rows, width = tokens.shape
    hidden = weight_in.shape[1]
    owners, cores = lax.axis_size(YZ), lax.axis_size("core")
    total = owners * rows

    w_in = jnp.concatenate([weight_in.T, swap(weight_in.T)], axis=0)
    w_out = jnp.concatenate([weight_out, swap(weight_out)], axis=0)

    both = spread(jnp.concatenate([tokens, grad_out], axis=1), YZ).reshape(total, 2 * width)
    parts = jnp.concatenate(
        [dot(both[:, :width], w_in, (1, 1)), dot(both[:, width:], w_out, (1, 1))], axis=1
    )
    pair = lax.all_gather(parts, "core", axis=0, tiled=False)
    half = total // cores
    mine = lax.dynamic_slice_in_dim(pair, lax.axis_index("core") * half, half, axis=1)
    share = jnp.sum(mine, axis=0)
    chip, chips = share.astype(BF), lax.axis_size("xh")
    for step in (2, 1, 3):
        perm = [(i, (i + step) % chips) for i in range(chips)]
        share = share + lax.ppermute(chip, "xh", perm).astype(F32)
    next_bias, _ = lax.optimization_barrier((bias_in, chip))
    bias = jnp.concatenate([bias_in, swap(next_bias)])
    acts_share, grad_pre_share = finish(share[:, : 2 * hidden], share[:, 2 * hidden :], bias)
    done = lax.all_gather(
        jnp.concatenate([acts_share, grad_pre_share], axis=1), "core", axis=0, tiled=True
    )
    acts, grad_pre = done[:, : 2 * hidden], done[:, 2 * hidden :]

    sums = jnp.concatenate([dot(acts, w_out, (1, 0)), dot(grad_pre, w_in, (1, 0))], axis=1)
    summed = jnp.sum(exchange(sums.astype(BF).reshape(owners, rows, 2 * width), YZ).astype(F32), axis=0)
    mixed = summed[:, :width].astype(BF)
    grad_tokens = summed[:, width:].astype(BF)

    their_tokens = swap(jnp.concatenate([both[:, :width], grad_pre[:, hidden:]], axis=1))
    their_grads = swap(jnp.concatenate([both[:, width:], acts[:, hidden:]], axis=1))
    all_pre = jnp.concatenate([grad_pre[:, :hidden], their_tokens[:, width:]], axis=0)
    all_tokens = jnp.concatenate([both[:, :width], their_tokens[:, :width]], axis=0)
    grad_weight_in = dot(all_tokens, all_pre, (0, 0)).astype(BF)
    grad_bias = jnp.sum(all_pre.astype(F32), axis=0)
    their_grads, grad_weight_in, grad_bias = lax.optimization_barrier(
        (their_grads, grad_weight_in, grad_bias)
    )
    all_acts = jnp.concatenate([acts[:, :hidden], their_grads[:, width:]], axis=0)
    all_grads = jnp.concatenate([both[:, width:], their_grads[:, :width]], axis=0)
    grad_weight_out = dot(all_acts, all_grads, (0, 0)).astype(BF)
    return (mixed, grad_tokens, grad_weight_in, grad_bias, grad_weight_out)


def solution(mesh):
    fine = Mesh(mesh.devices.reshape(tuple(AXES.values())), tuple(AXES))
    return jax.shard_map(
        body,
        mesh=fine,
        in_specs=(P(DP, MP), P(MP, DP), P(DP), P(DP, MP), P(DP, MP)),
        out_specs=(P(DP, MP), P(DP, MP), P(MP, DP), P(DP), P(DP, MP)),
        check_vma=False,
    )
```

```python
import jax
import jax.numpy as jnp
from jax import lax
from jax.sharding import Mesh, PartitionSpec as P

BF = jnp.bfloat16
F32 = jnp.float32

AXES = {"y": 8, "xl": 2, "z": 8, "xh": 4, "core": 2}
DP, MP = ("y", "xl", "z"), ("xh", "core")
YZ = ("y", "z")
SWAP = [(0, 1), (1, 0)]


def activation(values):
    return jax.nn.gelu(values, approximate=True)


def finish(pre_part, grad_part, bias_in):
    pre = pre_part + bias_in
    acts_full, backward = jax.vjp(activation, pre)
    grad_pre = backward(grad_part)[0]
    return (acts_full.astype(BF), grad_pre.astype(BF))


def exchange(blocks, axis):
    return lax.all_to_all(blocks, axis, split_axis=0, concat_axis=0, tiled=True)


def spread(block, axis):
    n = lax.axis_size(axis)
    return exchange(jnp.broadcast_to(block[None], (n, *block.shape)), axis)


def swap(block):
    return lax.ppermute(block, "xl", SWAP)


def dot(a, b, over):
    return lax.dot_general(a, b, ((over[:1], over[1:]), ((), ())), preferred_element_type=F32)


def body(tokens, weight_in, bias_in, weight_out, grad_out):
    rows, width = tokens.shape
    hidden = weight_in.shape[1]
    owners, cores = lax.axis_size(YZ), lax.axis_size("core")
    total = owners * rows

    w_in = jnp.concatenate([weight_in.T, swap(weight_in.T)], axis=0)
    w_out = jnp.concatenate([weight_out, swap(weight_out)], axis=0)
    bias = jnp.concatenate([bias_in, swap(bias_in)])

    both = spread(jnp.concatenate([tokens, grad_out], axis=1), YZ).reshape(total, 2 * width)
    parts = jnp.concatenate(
        [dot(both[:, :width], w_in, (1, 1)), dot(both[:, width:], w_out, (1, 1))], axis=1
    )
    pair = lax.all_gather(parts, "core", axis=0, tiled=False)
    half = total // cores
    mine = lax.dynamic_slice_in_dim(pair, lax.axis_index("core") * half, half, axis=1)
    share = jnp.sum(mine, axis=0)
    chip, chips = share.astype(BF), lax.axis_size("xh")
    for step in (2, 1, 3):
        perm = [(i, (i + step) % chips) for i in range(chips)]
        share = share + lax.ppermute(chip, "xh", perm).astype(F32)
    acts_share, grad_pre_share = finish(share[:, : 2 * hidden], share[:, 2 * hidden :], bias)
    done = lax.all_gather(
        jnp.concatenate([acts_share, grad_pre_share], axis=1), "core", axis=0, tiled=True
    )
    acts, grad_pre = done[:, : 2 * hidden], done[:, 2 * hidden :]

    sums = jnp.concatenate([dot(acts, w_out, (1, 0)), dot(grad_pre, w_in, (1, 0))], axis=1)
    summed = jnp.sum(exchange(sums.astype(BF).reshape(owners, rows, 2 * width), YZ).astype(F32), axis=0)
    mixed = summed[:, :width].astype(BF)
    grad_tokens = summed[:, width:].astype(BF)

    their_tokens = swap(jnp.concatenate([both[:, :width], grad_pre[:, hidden:]], axis=1))
    their_grads = swap(jnp.concatenate([both[:, width:], acts[:, hidden:]], axis=1))
    all_pre = jnp.concatenate([grad_pre[:, :hidden], their_tokens[:, width:]], axis=0)
    all_tokens = jnp.concatenate([both[:, :width], their_tokens[:, :width]], axis=0)
    grad_weight_in = dot(all_tokens, all_pre, (0, 0)).astype(BF)
    grad_bias = jnp.sum(all_pre.astype(F32), axis=0)
    their_grads, grad_weight_in, grad_bias = lax.optimization_barrier(
        (their_grads, grad_weight_in, grad_bias)
    )
    all_acts = jnp.concatenate([acts[:, :hidden], their_grads[:, width:]], axis=0)
    all_grads = jnp.concatenate([both[:, width:], their_grads[:, :width]], axis=0)
    grad_weight_out = dot(all_acts, all_grads, (0, 0)).astype(BF)
    return (mixed, grad_tokens, grad_weight_in, grad_bias, grad_weight_out)


def solution(mesh):
    fine = Mesh(mesh.devices.reshape(tuple(AXES.values())), tuple(AXES))
    return jax.shard_map(
        body,
        mesh=fine,
        in_specs=(P(DP, MP), P(MP, DP), P(DP), P(DP, MP), P(DP, MP)),
        out_specs=(P(DP, MP), P(DP, MP), P(MP, DP), P(DP), P(DP, MP)),
        check_vma=False,
    )
```

```python
import jax
import jax.numpy as jnp
from jax import lax
from jax.sharding import Mesh, PartitionSpec as P

BF = jnp.bfloat16
F32 = jnp.float32

AXES = {"y": 8, "xl": 2, "z": 8, "xh": 4, "core": 2}
DP, MP = ("y", "xl", "z"), ("xh", "core")
YZ = ("y", "z")
SWAP = [(0, 1), (1, 0)]


def activation(values):
    return jax.nn.gelu(values, approximate=True)


def finish(pre_part, grad_part, bias_in):
    pre = pre_part + bias_in
    acts_full, backward = jax.vjp(activation, pre)
    grad_pre = backward(grad_part)[0]
    return (acts_full.astype(BF), grad_pre.astype(BF))


def exchange(blocks, axis):
    return lax.all_to_all(blocks, axis, split_axis=0, concat_axis=0, tiled=True)


def spread(block, axis):
    n = lax.axis_size(axis)
    return exchange(jnp.broadcast_to(block[None], (n, *block.shape)), axis)


def swap(block):
    return lax.ppermute(block, "xl", SWAP)


def dot(a, b, over):
    return lax.dot_general(a, b, ((over[:1], over[1:]), ((), ())), preferred_element_type=F32)


def body(tokens, weight_in, bias_in, weight_out, grad_out):
    rows, width = tokens.shape
    hidden = weight_in.shape[1]
    owners, cores = lax.axis_size(YZ), lax.axis_size("core")
    total = owners * rows

    w_in = jnp.concatenate([weight_in.T, swap(weight_in.T)], axis=0)
    w_out = jnp.concatenate([weight_out, swap(weight_out)], axis=0)

    both = spread(jnp.concatenate([tokens, grad_out], axis=1), YZ).reshape(total, 2 * width)
    parts = jnp.concatenate(
        [dot(both[:, :width], w_in, (1, 1)), dot(both[:, width:], w_out, (1, 1))], axis=1
    )
    pair = lax.all_gather(parts, "core", axis=0, tiled=False)
    half = total // cores
    mine = lax.dynamic_slice_in_dim(pair, lax.axis_index("core") * half, half, axis=1)
    share = jnp.sum(mine, axis=0)
    chip, chips = share.astype(BF), lax.axis_size("xh")
    for step in (2, 3, 1):
        perm = [(i, (i + step) % chips) for i in range(chips)]
        share = share + lax.ppermute(chip, "xh", perm).astype(F32)
    next_bias, _ = lax.optimization_barrier((bias_in, chip))
    bias = jnp.concatenate([bias_in, swap(next_bias)])
    acts_share, grad_pre_share = finish(share[:, : 2 * hidden], share[:, 2 * hidden :], bias)
    done = lax.all_gather(
        jnp.concatenate([acts_share, grad_pre_share], axis=1), "core", axis=0, tiled=True
    )
    acts, grad_pre = done[:, : 2 * hidden], done[:, 2 * hidden :]

    sums = jnp.concatenate([dot(acts, w_out, (1, 0)), dot(grad_pre, w_in, (1, 0))], axis=1)
    summed = jnp.sum(exchange(sums.astype(BF).reshape(owners, rows, 2 * width), YZ).astype(F32), axis=0)
    mixed = summed[:, :width].astype(BF)
    grad_tokens = summed[:, width:].astype(BF)

    their_tokens = swap(jnp.concatenate([both[:, :width], grad_pre[:, hidden:]], axis=1))
    their_grads = swap(jnp.concatenate([both[:, width:], acts[:, hidden:]], axis=1))
    all_pre = jnp.concatenate([grad_pre[:, :hidden], their_tokens[:, width:]], axis=0)
    all_tokens = jnp.concatenate([both[:, :width], their_tokens[:, :width]], axis=0)
    grad_weight_in = dot(all_tokens, all_pre, (0, 0)).astype(BF)
    grad_bias = jnp.sum(all_pre.astype(F32), axis=0)
    their_grads, grad_weight_in, grad_bias = lax.optimization_barrier(
        (their_grads, grad_weight_in, grad_bias)
    )
    all_acts = jnp.concatenate([acts[:, :hidden], their_grads[:, width:]], axis=0)
    all_grads = jnp.concatenate([both[:, width:], their_grads[:, :width]], axis=0)
    grad_weight_out = dot(all_acts, all_grads, (0, 0)).astype(BF)
    return (mixed, grad_tokens, grad_weight_in, grad_bias, grad_weight_out)


def solution(mesh):
    fine = Mesh(mesh.devices.reshape(tuple(AXES.values())), tuple(AXES))
    return jax.shard_map(
        body,
        mesh=fine,
        in_specs=(P(DP, MP), P(MP, DP), P(DP), P(DP, MP), P(DP, MP)),
        out_specs=(P(DP, MP), P(DP, MP), P(MP, DP), P(DP), P(DP, MP)),
        check_vma=False,
    )
```
